32 devices in a mesh: dec: 16 (over z, y, x), tp: 2 (over core).
Axes of the slice: x: 2, y: 2, z: 4, core: 2. Of those that a mesh axis runs over, the one named last changes fastest.
Arguments:
- queries: bfloat16 [4, 128, 8192], P(None, 'dec', 'tp'), may hold values from -600 to 600
- new_kv: bfloat16 [4, 128, 2, 512], P(None, 'dec', None, 'tp'), may hold values from -6 to 6
- kv_pool: bfloat16 [1024, 32, 2, 512], P('dec', None, None, 'tp'), may hold values from -6 to 6
- block_table: int32 [128, 8], P('dec'), may hold values from 0 to 63, as said below
- lengths: int32 [128], P('dec'), may hold values from 1 to 252, as said below
- new_group: int32 [128], P('dec'), may hold values from 0 to 15, as said below
- hidden_rows: bfloat16 [4, 128, 4096], P(None, 'dec', 'tp'), may hold values from -6 to 6
- norm_gain: bfloat16 [4096], replicated, may hold values from 0.099609375 to 1.8984375
- routes: int32 [4, 128, 8], P(None, 'dec'), may hold values from 0 to 15, all different within a row; in each aligned block of 8 rows (0 to 7, 8 to 15, ..., all dimensions but the last counted through in order) at most 8 rows name the same one
- route_logits: float32 [4, 128, 8], P(None, 'dec'), may hold values from -2 to 301
- w_gate: bfloat16 [16, 4096, 1536], P('dec', None, 'tp'), may hold values from -0.09375 to 0.09375
- w_up: bfloat16 [16, 4096, 1536], P('dec', None, 'tp'), may hold values from -0.09375 to 0.09375
- w_down: bfloat16 [16, 1536, 4096], P('dec', 'tp'), may hold values from -0.15625 to 0.15625
Outputs:
- attn_out: bfloat16 [4, 128, 8192], P(None, 'dec', 'tp')
- moe_out: bfloat16 [4, 128, 4096], P(None, 'dec', 'tp')
- pool_after: bfloat16 [1024, 32, 2, 512], P('dec', None, None, 'tp')
The draws below stay inside these ranges and needn't reach their ends.
Inputs may be any that keep to these rules, and one draw needn't show every extreme that they name: `block_table`: within each group's 8 requests the table is a permutation of the group's 8 * 8 blocks. `lengths`: each group has a request of 252 tokens. `new_group`: in each group exactly one request names another group, all others name their own; the moves form one cycle through all groups, so each group receives exactly one request. `routes`: A request's 8 experts at a step are distinct; in one step the requests of one group name no expert more than 8 times.
All inputs are finite; a program needn't handle non-finite values.
Results may differ from the reference program's by a relative error of at most 0.0071.
Values may be sent and summed in bfloat16 or wider, within the bound.
A program may use at most 128 MiB of HBM per device.

```python
import math
import jax
import jax.numpy as jnp
import numpy as np
from jax import lax

D = 4096
FF = 1536
QH = 64
KVH = 4
HD = 128
TOP = 8
REQ_DEV = 8
BPR = 8
BT = 32
STEPS = 4
EXPERTS = 16
REQUESTS = 128
MAXLEN = 256
BLOCKS = 1024
CAP = 8
N_DEC = 16


def draw_queries(key, part):
    key = jax.random.fold_in(key, 11)
    base_draw = jnp.clip(jax.random.normal(key, (STEPS, REQUESTS, QH, HD), jnp.float32), -6.0, 6.0)
    return base_draw.reshape(STEPS, REQUESTS, QH * HD).astype(jnp.bfloat16)


def draw_route_logits(key, part):
    key = jax.random.fold_in(key, 12)
    return jnp.clip(0.5 * jax.random.normal(key, (STEPS, REQUESTS, TOP), jnp.float32), -2.0, 2.0)


def draw_lengths(key, part):
    key = jax.random.fold_in(key, 13)
    groups_all = REQUESTS // REQ_DEV
    longest = BT * BPR - STEPS
    values = jax.random.randint(key, (groups_all, REQ_DEV), 1, longest + 1)
    chosen_slot = jax.random.randint(jax.random.fold_in(key, 1), (groups_all, 1), 0, REQ_DEV)
    values = jnp.where(jnp.arange(REQ_DEV)[None, :] == chosen_slot, longest, values)
    return values.reshape(REQUESTS).astype(jnp.int32)


def draw_new_group(key, part):
    key = jax.random.fold_in(key, 14)
    groups_all = REQUESTS // REQ_DEV
    cycle_order = jax.random.permutation(key, groups_all)
    position_of = jnp.argsort(cycle_order)
    target_group = cycle_order[(position_of + 1) % groups_all]
    chosen_slot = jax.random.randint(jax.random.fold_in(key, 1), (groups_all, 1), 0, REQ_DEV)
    own_group = jnp.broadcast_to(jnp.arange(groups_all)[:, None], (groups_all, REQ_DEV))
    layout = jnp.where(jnp.arange(REQ_DEV)[None, :] == chosen_slot, target_group[:, None], own_group)
    return layout.reshape(REQUESTS).astype(jnp.int32)


def draw_block_table(key, part):
    key = jax.random.fold_in(key, 15)
    groups_all = REQUESTS // REQ_DEV
    per_group = REQ_DEV * BPR
    keys_list = jax.random.split(key, groups_all)
    tables = jax.vmap(lambda single: jax.random.permutation(single, per_group))(keys_list)
    return tables.reshape(REQUESTS, BPR).astype(jnp.int32)


def shard_levels(rng, extent, pieces, smallest, top_value):
    level, own = 1.0, jax.random.fold_in(rng, 6)
    for axis_at, parts in pieces:
        draws = jnp.exp(jax.random.uniform(jax.random.fold_in(own, axis_at), (parts,), jnp.float32, smallest / len(pieces), top_value / len(pieces)))
        level = level * jnp.repeat(draws, extent[axis_at] // parts).reshape([-1 if axis == axis_at else 1 for axis in range(len(extent))])
    return level


def deal_out(key, own, number, rows, count, top, bound, skew):
    sequence = jax.random.permutation(key, count)
    crowded, ordinary = load_shares(count, rows * top, bound, skew, True), load_shares(count, rows * top, bound, skew, False)
    places = jnp.arange(count)

    def named(sizes, rotation):
        used = int((sizes > 0).sum())
        fixed = max(1, used // 4)
        moved = fixed + (places - fixed + rotation * (used - fixed)) % max(1, count - fixed)
        return jnp.zeros((count,), jnp.int32).at[sequence[jnp.where(places < fixed, places, moved)]].set(jnp.asarray(sizes, jnp.int32))

    sizes = jnp.where(number % 4 == 0, named(crowded, number // 4), named(ordinary, number - number // 4 - 1))
    mixed = jax.random.permutation(jax.random.fold_in(own, 3), count)
    source_of, taker = mixed[0:count // 2 * 2:2], mixed[1:count // 2 * 2:2]
    room = jnp.minimum(sizes[source_of] - 1, bound - sizes[taker]) // 2
    room = jnp.where((source_of == sequence[0]) | (taker == sequence[0]) | (sizes[taker] == 0), 0, jnp.maximum(room, 0))
    moved = jax.random.randint(jax.random.fold_in(own, 4), (count // 2,), 0, 1 << 20) % (room + 1)
    sizes = sizes.at[source_of].add(-moved).at[taker].add(moved)
    items = jnp.searchsorted(jnp.cumsum(sizes), jnp.arange(rows * top), side="right").astype(jnp.int32)
    grid = items.reshape(top, rows).T
    grid = grid[jax.random.permutation(jax.random.fold_in(own, 1), rows)]
    rotation = jax.random.randint(jax.random.fold_in(own, 2), (rows, 1), 0, top)
    return jnp.take_along_axis(grid, (jnp.arange(top)[None, :] + rotation) % top, axis=1)


def load_shares(number_of, total, bound, lean, full):
    loads = [(1 << 20) // math.isqrt(grade ** lean) + 1 for grade in range(1, number_of + 1)]
    largest = bound if full else min(bound, max(-(-total // number_of), total * loads[0] // sum(loads)))
    least = 1 if total - largest >= number_of - 1 else 0
    holding, rest = [largest] + [least] * (number_of - 1), total - largest - least * (number_of - 1)
    while rest > 0:
        movable = [i for i in range(1, number_of) if holding[i] < largest] or [i for i in range(1, number_of) if holding[i] < bound]
        whole, budget = sum([loads[i] for i in movable]), rest
        for i in movable:
            more = min(bound - holding[i], max(1, budget * loads[i] // whole), rest)
            holding[i] = holding[i] + more
            rest = rest - more
    return np.array(holding)


def centred(stream_key, extent, deviation, limit, shards=(), held_as=jnp.bfloat16):
    entries = deviation * jax.random.normal(stream_key, extent, jnp.float32)
    if shards:
        entries = entries * shard_levels(stream_key, extent, shards, -0.22, 0.18)
    return jnp.clip(entries, -limit, limit).astype(held_as)


def setup_inputs(seed: int = 0) -> dict:
    key_list = jax.random.split(jax.random.key(seed), 14)
    queries = draw_queries(jax.random.fold_in(key_list[13], 71), 0)
    new_kv = centred(key_list[1], (STEPS, REQUESTS, 2, KVH * HD), 1.0, 6.0, ((1, 16), (3, 2)))
    kv_pool = centred(key_list[2], (BLOCKS, BT, 2, KVH * HD), 1.0, 6.0, ((0, 16), (3, 2)))
    block_table = draw_block_table(jax.random.fold_in(key_list[13], 71), 0)
    lengths = draw_lengths(jax.random.fold_in(key_list[13], 71), 0)
    new_group = draw_new_group(jax.random.fold_in(key_list[13], 71), 0)
    hidden_rows = centred(key_list[6], (STEPS, REQUESTS, D), 1.0, 6.0, ((1, 16), (2, 2)))
    norm_gain = jnp.clip(1.0 + 0.18 * jax.random.normal(key_list[7], (D,), jnp.float32), 0.099609375, 1.8984375).astype(jnp.bfloat16)
    routes_keys = jax.random.split(jax.random.fold_in(key_list[8], 1), STEPS * REQUESTS // REQ_DEV)
    routes_turns = jax.random.permutation(jax.random.fold_in(key_list[8], 3), STEPS * REQUESTS // REQ_DEV)
    routes = jax.vmap(lambda own, number: deal_out(jax.random.fold_in(key_list[8], 2), own, number, REQ_DEV, EXPERTS, TOP, CAP, 2))(routes_keys, routes_turns).reshape((STEPS, REQUESTS, TOP))
    route_logits = draw_route_logits(jax.random.fold_in(key_list[13], 71), 0)
    w_gate = centred(key_list[10], (EXPERTS, D, FF), D ** -0.5, 0.09375, ((0, 16), (2, 2)))
    w_up = centred(key_list[11], (EXPERTS, D, FF), D ** -0.5, 0.09375, ((0, 16), (2, 2)))
    w_down = centred(key_list[12], (EXPERTS, FF, D), FF ** -0.5, 0.15625, ((0, 16), (1, 2)))
    return {"queries": queries, "new_kv": new_kv, "kv_pool": kv_pool, "block_table": block_table, "lengths": lengths, "new_group": new_group, "hidden_rows": hidden_rows, "norm_gain": norm_gain, "routes": routes, "route_logits": route_logits, "w_gate": w_gate, "w_up": w_up, "w_down": w_down}


eps_norm = 1e-06

def rms_scaled(values, gain_vec):
    widened = values.astype(jnp.float32)
    factor = lax.rsqrt(lax.optimization_barrier(jnp.mean(widened * widened, axis=-1, keepdims=True)) + eps_norm)
    return (widened * factor * gain_vec.astype(jnp.float32)).astype(jnp.bfloat16)

def attend_step(query_rows, keys_all, values_all, lengths, step_index):
    row_count, cache_span, kv_local, head_dim = keys_all.shape
    group_ratio = query_rows.shape[1] // (kv_local * head_dim)
    grouped = query_rows.reshape(row_count, kv_local, group_ratio, head_dim).astype(jnp.float32)
    scores = jnp.einsum('rkgd,rlkd->rkgl', grouped, keys_all.astype(jnp.float32))
    scores = scores * (1.0 / math.sqrt(head_dim))
    visible = jnp.arange(cache_span)[None, :] < (lengths + step_index + 1)[:, None]
    visible = visible[:, None, None, :]
    masked = jnp.where(visible, scores, -1e+30)
    highest = lax.optimization_barrier(jnp.max(masked, axis=-1, keepdims=True))
    weights = jnp.where(visible, jnp.exp(masked - highest), 0.0)
    weight_sum = lax.optimization_barrier(jnp.sum(weights, axis=-1, keepdims=True))
    shares = (weights / weight_sum).astype(jnp.bfloat16)
    mixed_out = jnp.einsum('rkgl,rlkd->rkgd', shares.astype(jnp.float32), values_all.astype(jnp.float32))
    return mixed_out.astype(jnp.bfloat16).reshape(row_count, -1)

def expert_block(operands):
    expert_rows, gate_mat, up_mat, down_mat = operands
    gate_out = jnp.dot(expert_rows, gate_mat, preferred_element_type=jnp.float32)
    up_out = jnp.dot(expert_rows, up_mat, preferred_element_type=jnp.float32)
    inner_act = (jax.nn.silu(gate_out) * up_out).astype(jnp.bfloat16)
    return jnp.dot(inner_act, down_mat, preferred_element_type=jnp.float32).astype(jnp.bfloat16)

def reference(queries, new_kv, kv_pool, block_table, lengths, new_group, hidden_rows, norm_gain, routes, route_logits, w_gate, w_up, w_down):
    blocks_dev = REQ_DEV * BPR
    request_ids = jnp.arange(REQUESTS, dtype=jnp.int32)
    owner_group = request_ids // REQ_DEV
    global_table = block_table + (owner_group * blocks_dev)[:, None]
    flat_pool = kv_pool.reshape(BLOCKS * BT, 2, KVH * HD)
    for step_index in range(STEPS):
        position = lengths + step_index
        target_rows = global_table[request_ids, position // BT] * BT + position % BT
        flat_pool = flat_pool.at[target_rows].set(new_kv[step_index])
    pool_now = flat_pool.reshape(BLOCKS, BT, 2, KVH * HD)
    cached = pool_now[global_table].reshape(REQUESTS, MAXLEN, 2, KVH, HD)
    keys_all = cached[:, :, 0]
    values_all = cached[:, :, 1]
    attn_out = jnp.stack([attend_step(queries[step_index], keys_all, values_all, lengths, step_index) for step_index in range(STEPS)])
    leaving = (new_group != owner_group).astype(jnp.int32).reshape(N_DEC, REQ_DEV)
    depart_req = jnp.arange(N_DEC, dtype=jnp.int32) * REQ_DEV + jnp.argmax(leaving, axis=1).astype(jnp.int32)
    destination = new_group[depart_req]
    group_ids = jnp.arange(N_DEC, dtype=jnp.int32)
    source = jnp.argmax((destination[None, :] == group_ids[:, None]).astype(jnp.int32), axis=1).astype(jnp.int32)
    depart_blocks = global_table[depart_req]
    incoming = pool_now[depart_blocks[source]]
    pool_after = pool_now.at[depart_blocks.reshape(-1)].set(incoming.reshape(N_DEC * BPR, BT, 2, KVH * HD))
    route_ids = routes.reshape(STEPS, N_DEC, REQ_DEV * TOP)
    hits_table = (route_ids[..., None] == jnp.arange(EXPERTS, dtype=jnp.int32)).astype(jnp.int32)
    earlier = jnp.cumsum(hits_table, axis=2) - hits_table
    placing = lax.optimization_barrier(jnp.sum(earlier * hits_table, axis=-1))
    step_ids = jnp.arange(STEPS, dtype=jnp.int32)[:, None, None]
    group_col = group_ids[None, :, None]
    slot_index = (((route_ids * STEPS + step_ids) * N_DEC + group_col) * CAP + placing).reshape(-1)
    normed = rms_scaled(hidden_rows, norm_gain)
    spread_rows = jnp.repeat(normed, TOP, axis=1)
    buffer = jnp.zeros((EXPERTS * STEPS * N_DEC * CAP, D), jnp.bfloat16).at[slot_index].set(spread_rows.reshape(-1, D))
    expert_out = lax.map(expert_block, (buffer.reshape(EXPERTS, STEPS * N_DEC * CAP, D), w_gate, w_up, w_down))
    picked = expert_out.reshape(-1, D)[slot_index].astype(jnp.float32).reshape(STEPS, REQUESTS, TOP, D)
    route_probs = jax.nn.softmax(route_logits, axis=-1)
    moe_out = lax.optimization_barrier(jnp.sum(picked * route_probs[..., None], axis=2)).astype(jnp.bfloat16)
    return (attn_out, moe_out, pool_after)
```

```python
import math

import jax
import jax.numpy as jnp
from jax import lax
from jax.experimental import pallas as pl
from jax.experimental.pallas import tpu as pltpu
from jax.sharding import PartitionSpec as P

HD = 128


eps_norm = 1e-06


def rms_scaled(values, gain_vec):
    widened = values.astype(jnp.float32)
    factor = lax.rsqrt(jnp.mean(widened * widened, axis=-1, keepdims=True) + eps_norm)
    return (widened * factor * gain_vec.astype(jnp.float32)).astype(jnp.bfloat16)


def attend_step(query_rows, keys_all, values_all, lengths, step_index):
    row_count, cache_span, kv_local, head_dim = keys_all.shape
    group_ratio = query_rows.shape[1] // (kv_local * head_dim)
    grouped = query_rows.reshape(row_count, kv_local, group_ratio, head_dim)
    scores = jnp.einsum("rkgd,rlkd->rkgl", grouped, keys_all, preferred_element_type=jnp.float32)
    scores = scores * (1.0 / math.sqrt(head_dim))
    visible = jnp.arange(cache_span)[None, :] < (lengths + step_index + 1)[:, None]
    visible = visible[:, None, None, :]
    masked = jnp.where(visible, scores, -1e30)
    highest = jnp.max(masked, axis=-1, keepdims=True)
    weights = jnp.where(visible, jnp.exp(masked - highest), 0.0)
    weight_sum = jnp.sum(weights, axis=-1, keepdims=True)
    shares = (weights / weight_sum).astype(jnp.bfloat16)
    mixed_out = jnp.einsum(
        "rkgl,rlkd->rkgd", shares, values_all, preferred_element_type=jnp.float32
    )
    return mixed_out.astype(jnp.bfloat16).reshape(row_count, -1)


def slot_layout(route_ids, experts_all, capacity):
    flat_ids = route_ids.reshape(-1)
    hits_table = (flat_ids[:, None] == jnp.arange(experts_all)[None, :]).astype(jnp.int32)
    earlier = jnp.cumsum(hits_table, axis=0) - hits_table
    placing = jnp.sum(earlier * hits_table, axis=1)
    return flat_ids * capacity + placing


def expert_apply(normed, w_gate, w_up, w_down):
    flat_rows = normed.reshape(-1, normed.shape[-1])
    gate_out = jnp.dot(flat_rows, w_gate[0], preferred_element_type=jnp.float32)
    up_out = jnp.dot(flat_rows, w_up[0], preferred_element_type=jnp.float32)
    inner_act = (jax.nn.silu(gate_out) * up_out).astype(jnp.bfloat16)
    partial_value = jnp.dot(inner_act, w_down[0], preferred_element_type=jnp.float32)
    partial_value = partial_value.reshape(normed.shape[0], normed.shape[1], -1)
    summed = lax.psum_scatter(partial_value, "tp", scatter_dimension=2, tiled=True).astype(
        jnp.bfloat16
    )
    return lax.all_to_all(summed, "dec", split_axis=0, concat_axis=0, tiled=True)


def body_general(
    queries,
    new_kv,
    kv_pool,
    block_table,
    lengths,
    new_group,
    hidden_rows,
    norm_gain,
    routes,
    route_logits,
    w_gate,
    w_up,
    w_down,
):
    step_total = new_kv.shape[0]
    req_local = new_kv.shape[1]
    kv_width = new_kv.shape[3]
    block_local = kv_pool.shape[0]
    block_tokens = kv_pool.shape[1]
    blocks_per = block_table.shape[1]
    span_total = blocks_per * block_tokens
    kv_local = kv_width // HD
    request_ids = jnp.arange(req_local)
    flat_pool = kv_pool.reshape(block_local * block_tokens, 2, kv_width)
    for step_index in range(step_total):
        position = lengths + step_index
        target_rows = (
            block_table[request_ids, position // block_tokens] * block_tokens
            + position % block_tokens
        )
        flat_pool = flat_pool.at[target_rows].set(new_kv[step_index])
    pool_now = flat_pool.reshape(block_local, block_tokens, 2, kv_width)
    cached = pool_now[block_table].reshape(req_local, span_total, 2, kv_local, HD)
    keys_all = cached[:, :, 0]
    values_all = cached[:, :, 1]
    attn_out = jnp.stack(
        [
            attend_step(queries[step_index], keys_all, values_all, lengths, step_index)
            for step_index in range(step_total)
        ]
    )
    group_self = lax.axis_index("dec")
    group_count = lax.axis_size("dec")
    leaving = (new_group != group_self).astype(jnp.int32)
    depart_slot = jnp.argmax(leaving)
    destination = new_group[depart_slot]
    depart_blocks = block_table[depart_slot]
    outgoing = pool_now[depart_blocks].reshape(span_total, 2, kv_width)
    every_cache, every_dest = (
        lax.all_gather(outgoing[None], "dec", axis=0, tiled=True),
        lax.all_gather(destination.reshape(1), "dec", axis=0, tiled=True),
    )
    source = jnp.argmax((every_dest == group_self).astype(jnp.int32))
    incoming = lax.dynamic_index_in_dim(every_cache, source, 0, keepdims=False)
    pool_after = pool_now.at[depart_blocks].set(
        incoming.reshape(blocks_per, block_tokens, 2, kv_width)
    )
    top_count = routes.shape[2]
    capacity = min(req_local, 2 * ((req_local * top_count + group_count - 1) // group_count))
    owners = jnp.repeat(request_ids, top_count)
    moe_list = []
    for step_index in range(step_total):
        slot_index = slot_layout(routes[step_index], group_count, capacity)
        route_probs = jax.nn.softmax(route_logits[step_index], axis=-1)
        local_rows = hidden_rows[step_index]
        buffer = (
            jnp.zeros((group_count * capacity, local_rows.shape[1]), jnp.bfloat16)
            .at[slot_index]
            .set(local_rows[owners])
        )
        full_rows = lax.all_gather(
            lax.all_to_all(
                buffer.reshape(group_count, capacity, -1),
                "dec",
                split_axis=0,
                concat_axis=0,
                tiled=True,
            ),
            "tp",
            axis=2,
            tiled=True,
        )
        returned_rows = expert_apply(rms_scaled(full_rows, norm_gain), w_gate, w_up, w_down)
        picked = returned_rows.reshape(group_count * capacity, -1)[slot_index].astype(jnp.float32)
        weighted = picked * route_probs.reshape(-1, 1)
        moe_list.append(
            jnp.sum(weighted.reshape(req_local, top_count, -1), axis=1).astype(jnp.bfloat16)
        )
    moe_out = jnp.stack(moe_list)
    return (attn_out, moe_out, pool_after)


MESH = pl.DeviceIdType.MESH
F32 = jnp.float32
BF = jnp.bfloat16
SS, ZG, X1, Y1, X2, Y2, SIB, TP, RA, RB, RA2, RB2, RZ = range(13)
PIECE = 16


def exchange_kernel(
    hid, gain, routes, logits, out_cache, wg_hbm, wu_hbm, wd_hbm,
    moe_ref, inc_ref,
    wg, wu, wd, gath, ss_out, ss_in, act, acc, tp_out, tp_in,
    a_out, a_in, b_out, b_in, a2_out, a2_in, b2_out, b2_in, z_out, z_in,
    mig_in, mig_out, wsem, ssem, rsem, m_s1, m_r1, m_s2, m_r2, local_sem,
):
    me = lax.axis_index("dec")
    core = lax.axis_index("tp")
    x, y, z = me % 2, (me // 2) % 2, me // 4
    x_peer = me + 1 - 2 * x
    y_peer = me + 2 - 4 * y
    z_peers = [me, me + 4 - 8 * (z % 2), ((z + 2) % 4) * 4 + me % 4, (3 - z) * 4 + me % 4]
    half = hid.shape[2]
    quarter = half // 2
    count = 16

    barrier = pltpu.get_barrier_semaphore()
    for m in range(1, count):
        pl.semaphore_signal(barrier, inc=1, device_id={"dec": (me + m) % count}, device_id_type=MESH)
    pl.semaphore_signal(barrier, inc=1, device_id={"tp": 1 - core}, device_id_type=MESH)

    weights = [
        pltpu.make_async_copy(src.at[0], dst, wsem.at[i])
        for i, (src, dst) in enumerate(((wg_hbm, wg), (wu_hbm, wu), (wd_hbm, wd)))
    ]
    for copy in weights:
        copy.start()

    raw = jnp.concatenate([hid[t].astype(F32) for t in range(hid.shape[0])], axis=0)
    own_sum = jnp.sum(raw * raw, axis=-1, keepdims=True)
    ss_out[...] = jnp.broadcast_to(own_sum, ss_out.shape)
    pl.semaphore_wait(barrier, count)

    def remote(kind, q, src, dst, peer):
        return pltpu.make_async_remote_copy(
            src_ref=src, dst_ref=dst, send_sem=ssem.at[kind, q], recv_sem=rsem.at[kind, q],
            device_id=peer, device_id_type=MESH,
        )

    ss_copy = remote(SS, 0, ss_out, ss_in, {"tp": 1 - core})
    ss_copy.start()

    lane = lax.broadcasted_iota(jnp.int32, (raw.shape[0], 128), 1)
    logit = jnp.concatenate([logits[t] for t in range(hid.shape[0])], axis=0)
    route = jnp.concatenate([routes[t] for t in range(hid.shape[0])], axis=0)
    grown = jnp.exp(logit - jnp.max(logit, axis=-1, keepdims=True))
    prob = grown / jnp.sum(grown, axis=-1, keepdims=True)
    dense = jnp.zeros(lane.shape, F32)
    for k in range(route.shape[1]):
        hit = (lane % 16) == route[:, k : k + 1]
        dense = dense + jnp.where(hit, prob[:, k : k + 1], 0.0)
    high = dense.astype(BF)
    low = (dense - high.astype(F32)).astype(BF)
    packed = jnp.where(lane < 16, high.astype(F32), low.astype(F32)).astype(BF)

    ss_copy.wait()
    total = own_sum + ss_in[:, 0:1]
    factor = lax.rsqrt(total * (1.0 / (2 * half)) + eps_norm)
    own_gain = jnp.where(core == 0, gain[0:1], gain[1:2])
    rows = raw.shape[0]
    gath[core, 0, 0:rows, 0:half] = (raw * factor * own_gain).astype(BF)
    gath[core, 0, 0:rows, half:] = packed

    def slot(q, j, lo=0, hi=None):
        return gath.at[core, q, pl.ds(j * rows, rows), pl.ds(lo, (hi or gath.shape[3]) - lo)]

    sends = []

    def go(copy):
        copy.start()
        sends.append(copy)
        return copy

    x1, y1 = {}, {}

    def spread(q):
        x1[q] = go(remote(X1, q, slot(q, 0), slot(q, 1), {"dec": x_peer}))
        y1[q] = go(remote(Y1, q, slot(q, 0), slot(q, 2), {"dec": y_peer}))

    spread(0)
    zg = {q: go(remote(ZG, q, slot(0, 0), slot(q, 0), {"dec": z_peers[q]})) for q in (1, 2, 3)}

    first = []
    for m in range(1, count):
        peer = (me + m) % count
        copy = pltpu.make_async_remote_copy(
            src_ref=out_cache.at[pl.ds(peer * PIECE, PIECE)], dst_ref=mig_in.at[m],
            send_sem=m_s1.at[m], recv_sem=m_r1.at[m], device_id={"dec": peer}, device_id_type=MESH,
        )
        copy.start()
        first.append(copy)
    mig_in[0] = out_cache[pl.ds(me * PIECE, PIECE)]

    def gather(q):
        if q < 3:
            zg[q + 1].wait_recv()
            spread(q + 1)
        y1[q].wait_recv()
        x2 = go(remote(X2, q, slot(q, 2, 0, quarter), slot(q, 3, 0, quarter), {"dec": x_peer}))
        x1[q].wait_recv()
        y2 = go(remote(Y2, q, slot(q, 1, quarter), slot(q, 3, quarter), {"dec": y_peer}))
        x2.wait_recv()
        y2.wait_recv()
        return go(remote(SIB, q, gath.at[core, q], gath.at[core, q], {"tp": 1 - core}))

    def apply(q):
        if q == 0:
            weights[0].wait()
            weights[1].wait()

        @pl.loop(0, act.shape[1] // 256)
        def _(i):
            cols = pl.ds(pl.multiple_of(i * 256, 256), 256)

            def product(w):
                return jnp.dot(
                    gath[0, q, :, 0:half], w[0:half, cols], preferred_element_type=F32
                ) + jnp.dot(
                    gath[1, q, :, 0:half], w[half : 2 * half, cols], preferred_element_type=F32
                )

            g = product(wg)
            act[:, cols] = (g / (1.0 + jnp.exp(-g)) * product(wu)).astype(BF)

        if q == 0:
            weights[2].wait()
        probs = gath[0, q, :, half:].astype(F32)
        lanes = lax.broadcasted_iota(jnp.int32, probs.shape, 1)
        mine = (lanes == me) | (lanes == me + 16)
        weight = jnp.sum(jnp.where(mine, probs, 0.0), axis=-1, keepdims=True)
        step = 512

        @pl.loop(0, half // step)
        def _(i):
            to = pl.ds(pl.multiple_of(i * step, step), step)
            cols = pl.ds(pl.multiple_of((1 - core) * half + i * step, step), step)
            tp_out[q, :, to] = (
                jnp.dot(act[...], wd[:, cols], preferred_element_type=F32) * weight
            ).astype(BF)

        copy = go(remote(TP, q, tp_out.at[q], tp_in.at[q], {"tp": 1 - core}))

        @pl.loop(0, half // step)
        def _(i):
            to = pl.ds(pl.multiple_of(i * step, step), step)
            cols = pl.ds(pl.multiple_of(core * half + i * step, step), step)
            acc[q, :, to] = jnp.dot(act[...], wd[:, cols], preferred_element_type=F32) * weight

        return copy

    ra, rb, ra2, rb2, rz = {}, {}, {}, {}, {}
    r = rows

    def fold1(q, copy):
        copy.wait_recv()
        acc[q] = acc[q] + tp_in[q].astype(F32)
        a_out[q, 0:r] = acc[q, r : 2 * r, 0:quarter].astype(BF)
        a_out[q, r : 2 * r] = acc[q, 3 * r : 4 * r, 0:quarter].astype(BF)
        ra[q] = go(remote(RA, q, a_out.at[q], a_in.at[q], {"dec": x_peer}))
        b_out[q] = acc[q, 2 * r : 4 * r, quarter:].astype(BF)
        rb[q] = go(remote(RB, q, b_out.at[q], b_in.at[q], {"dec": y_peer}))

    def fold2(q):
        ra[q].wait_recv()
        a2_out[q] = (acc[q, 2 * r : 3 * r, 0:quarter] + a_in[q, r : 2 * r].astype(F32)).astype(BF)
        ra2[q] = go(remote(RA2, q, a2_out.at[q], a2_in.at[q], {"dec": y_peer}))
        rb[q].wait_recv()
        b2_out[q] = (acc[q, r : 2 * r, quarter:] + b_in[q, r : 2 * r].astype(F32)).astype(BF)
        rb2[q] = go(remote(RB2, q, b2_out.at[q], b2_in.at[q], {"dec": x_peer}))
        acc[q, 0:r, 0:quarter] = acc[q, 0:r, 0:quarter] + a_in[q, 0:r].astype(F32)
        acc[q, 0:r, quarter:] = acc[q, 0:r, quarter:] + b_in[q, 0:r].astype(F32)

    def fold3(q):
        ra2[q].wait_recv()
        rb2[q].wait_recv()
        acc[q, 0:r, 0:quarter] = acc[q, 0:r, 0:quarter] + a2_in[q].astype(F32)
        acc[q, 0:r, quarter:] = acc[q, 0:r, quarter:] + b2_in[q].astype(F32)
        if q:
            z_out[q] = acc[q, 0:r].astype(BF)
            rz[q] = go(remote(RZ, q, z_out.at[q], z_in.at[q], {"dec": z_peers[q]}))

    sib = gather(0)
    for copy in first:
        copy.wait()
    width = mig_out.shape[2]
    second = []
    for m in range(count):
        peer = (me + m) % count
        wanted = peer.astype(F32)
        chosen = jnp.zeros((PIECE, width), F32)
        for n in range(count):
            head = mig_in[n, :, width : width + 1].astype(F32)
            chosen = jnp.where(head == wanted, mig_in[n, :, 0:width].astype(F32), chosen)
        mig_out[m] = chosen.astype(BF)
        where = inc_ref.at[pl.ds(me * PIECE, PIECE)]
        if m:
            copy = pltpu.make_async_remote_copy(
                src_ref=mig_out.at[m], dst_ref=where, send_sem=m_s2.at[m], recv_sem=m_r2.at[m],
                device_id={"dec": peer}, device_id_type=MESH,
            )
        else:
            copy = pltpu.make_async_copy(mig_out.at[m], where, local_sem)
        copy.start()
        second.append(copy)

    sib.wait_recv()
    tp0 = apply(0)
    sib = gather(1)
    fold1(0, tp0)
    sib.wait_recv()
    tp1 = apply(1)
    fold2(0)
    sib = gather(2)
    fold1(1, tp1)
    fold3(0)
    sib.wait_recv()
    tp2 = apply(2)
    fold2(1)
    sib = gather(3)
    fold1(2, tp2)
    fold3(1)
    sib.wait_recv()
    tp3 = apply(3)
    fold2(2)
    fold1(3, tp3)
    fold3(2)
    fold2(3)
    for copy in second:
        copy.wait()
    fold3(3)
    result = acc[0, 0:r]
    for q in (1, 2, 3):
        rz[q].wait_recv()
        result = result + z_in[q].astype(F32)
    for t in range(moe_ref.shape[0]):
        moe_ref[t] = result[t * 8 : t * 8 + 8].astype(BF)
    for copy in sends:
        copy.wait_send()


def exchange(hidden, gain, routes, logits, out_cache, w_gate, w_up, w_down):
    steps, req, half = hidden.shape
    rows = steps * req
    quarter = half // 2
    wide = w_gate.shape[2]
    vm = pltpu.VMEM
    scratch = [
        vm(w_gate.shape[1:], BF), vm(w_up.shape[1:], BF), vm(w_down.shape[1:], BF),
        vm((2, 4, 4 * rows, half + 128), BF),
        vm((rows, 128), F32), vm((rows, 128), F32),
        vm((4 * rows, wide), BF),
        vm((4, 4 * rows, half), F32),
        vm((4, 4 * rows, half), BF), vm((4, 4 * rows, half), BF),
        vm((4, 2 * rows, quarter), BF), vm((4, 2 * rows, quarter), BF),
        vm((4, 2 * rows, quarter), BF), vm((4, 2 * rows, quarter), BF),
        vm((4, rows, quarter), BF), vm((4, rows, quarter), BF),
        vm((4, rows, quarter), BF), vm((4, rows, quarter), BF),
        vm((4, rows, half), BF), vm((4, rows, half), BF),
        vm((16, PIECE, out_cache.shape[1]), BF), vm((16, PIECE, out_cache.shape[1] - 128), BF),
        pltpu.SemaphoreType.DMA((3,)),
        pltpu.SemaphoreType.DMA((13, 4)), pltpu.SemaphoreType.DMA((13, 4)),
        pltpu.SemaphoreType.DMA((16,)), pltpu.SemaphoreType.DMA((16,)),
        pltpu.SemaphoreType.DMA((16,)), pltpu.SemaphoreType.DMA((16,)),
        pltpu.SemaphoreType.DMA,
    ]
    inside = pl.BlockSpec(memory_space=pltpu.VMEM)
    outside = pl.BlockSpec(memory_space=pl.ANY)
    return pl.pallas_call(
        exchange_kernel,
        out_shape=(
            jax.ShapeDtypeStruct((steps, req, half), BF),
            jax.ShapeDtypeStruct((out_cache.shape[0], out_cache.shape[1] - 128), BF),
        ),
        in_specs=[inside] * 5 + [outside] * 3,
        out_specs=(inside, inside),
        scratch_shapes=scratch,
        compiler_params=pltpu.CompilerParams(
            collective_id=0, has_side_effects=True, vmem_limit_bytes=56 * 1024 * 1024
        ),
    )(hidden, gain, routes, logits, out_cache, w_gate, w_up, w_down)


def body_slots(
    queries, new_kv, kv_pool, block_table, lengths, new_group, hidden_rows, norm_gain,
    routes, route_logits, w_gate, w_up, w_down,
):
    steps, req, _, kv_width = new_kv.shape
    blocks, block_tokens = kv_pool.shape[:2]
    span = block_table.shape[1] * block_tokens
    kv_local = kv_width // HD
    position = lengths[None, :] + jnp.arange(steps)[:, None]
    target = (
        block_table[jnp.arange(req)[None, :], position // block_tokens] * block_tokens
        + position % block_tokens
    )
    pool_now = (
        kv_pool.reshape(blocks * block_tokens, 2, kv_width)
        .at[target.reshape(-1)]
        .set(new_kv.reshape(steps * req, 2, kv_width))
        .reshape(kv_pool.shape)
    )
    slot = jnp.argmax((new_group != lax.axis_index("dec")).astype(jnp.int32))
    depart = block_table[slot]
    outgoing = pool_now[depart].reshape(span, 2 * kv_width)
    head = jnp.broadcast_to(new_group[slot].astype(BF), (span, 128))
    moe_out, incoming = exchange(
        hidden_rows, norm_gain.astype(F32).reshape(2, -1), routes, route_logits,
        jnp.concatenate([outgoing, head], axis=1), w_gate, w_up, w_down,
    )
    cached = pool_now[block_table].reshape(req, span, 2, kv_local, HD)
    keys, values = cached[:, :, 0], cached[:, :, 1]
    grouped = queries.reshape(steps, req, kv_local, -1, HD)
    scores = jnp.einsum("trkgd,rlkd->rktgl", grouped, keys, preferred_element_type=F32)
    scores = scores * (1.0 / math.sqrt(HD))
    visible = jnp.arange(span)[None, None, :] < (position.T + 1)[:, :, None]
    visible = visible[:, None, :, None, :]
    masked = jnp.where(visible, scores, -1e30)
    weights = jnp.where(visible, jnp.exp(masked - jnp.max(masked, axis=-1, keepdims=True)), 0.0)
    shares = (weights / jnp.sum(weights, axis=-1, keepdims=True)).astype(BF)
    mixed = jnp.einsum("rktgl,rlkd->trkgd", shares, values, preferred_element_type=F32)
    attn_out = mixed.astype(BF).reshape(steps, req, -1)
    pool_after = pool_now.at[depart].set(incoming.reshape(-1, block_tokens, 2, kv_width))
    return attn_out, moe_out, pool_after


def solution(mesh):
    sized = mesh.shape["dec"] == 16 and mesh.shape["tp"] == 2
    body = body_slots if sized else body_general
    return jax.shard_map(
        body,
        mesh=mesh,
        in_specs=(
            P(None, "dec", "tp"),
            P(None, "dec", None, "tp"),
            P("dec", None, None, "tp"),
            P("dec", None),
            P("dec"),
            P("dec"),
            P(None, "dec", "tp"),
            P(),
            P(None, "dec", None),
            P(None, "dec", None),
            P("dec", None, "tp"),
            P("dec", None, "tp"),
            P("dec", "tp", None),
        ),
        out_specs=(P(None, "dec", "tp"), P(None, "dec", "tp"), P("dec", None, None, "tp")),
        check_vma=False,
    )
```

```python
import math

import jax
import jax.numpy as jnp
from jax import lax
from jax.experimental import pallas as pl
from jax.experimental.pallas import tpu as pltpu
from jax.sharding import PartitionSpec as P

HD = 128


eps_norm = 1e-06


def rms_scaled(values, gain_vec):
    widened = values.astype(jnp.float32)
    factor = lax.rsqrt(jnp.mean(widened * widened, axis=-1, keepdims=True) + eps_norm)
    return (widened * factor * gain_vec.astype(jnp.float32)).astype(jnp.bfloat16)


def attend_step(query_rows, keys_all, values_all, lengths, step_index):
    row_count, cache_span, kv_local, head_dim = keys_all.shape
    group_ratio = query_rows.shape[1] // (kv_local * head_dim)
    grouped = query_rows.reshape(row_count, kv_local, group_ratio, head_dim)
    scores = jnp.einsum("rkgd,rlkd->rkgl", grouped, keys_all, preferred_element_type=jnp.float32)
    scores = scores * (1.0 / math.sqrt(head_dim))
    visible = jnp.arange(cache_span)[None, :] < (lengths + step_index + 1)[:, None]
    visible = visible[:, None, None, :]
    masked = jnp.where(visible, scores, -1e30)
    highest = jnp.max(masked, axis=-1, keepdims=True)
    weights = jnp.where(visible, jnp.exp(masked - highest), 0.0)
    weight_sum = jnp.sum(weights, axis=-1, keepdims=True)
    shares = (weights / weight_sum).astype(jnp.bfloat16)
    mixed_out = jnp.einsum(
        "rkgl,rlkd->rkgd", shares, values_all, preferred_element_type=jnp.float32
    )
    return mixed_out.astype(jnp.bfloat16).reshape(row_count, -1)


def slot_layout(route_ids, experts_all, capacity):
    flat_ids = route_ids.reshape(-1)
    hits_table = (flat_ids[:, None] == jnp.arange(experts_all)[None, :]).astype(jnp.int32)
    earlier = jnp.cumsum(hits_table, axis=0) - hits_table
    placing = jnp.sum(earlier * hits_table, axis=1)
    return flat_ids * capacity + placing


def expert_apply(normed, w_gate, w_up, w_down):
    flat_rows = normed.reshape(-1, normed.shape[-1])
    gate_out = jnp.dot(flat_rows, w_gate[0], preferred_element_type=jnp.float32)
    up_out = jnp.dot(flat_rows, w_up[0], preferred_element_type=jnp.float32)
    inner_act = (jax.nn.silu(gate_out) * up_out).astype(jnp.bfloat16)
    partial_value = jnp.dot(inner_act, w_down[0], preferred_element_type=jnp.float32)
    partial_value = partial_value.reshape(normed.shape[0], normed.shape[1], -1)
    summed = lax.psum_scatter(partial_value, "tp", scatter_dimension=2, tiled=True).astype(
        jnp.bfloat16
    )
    return lax.all_to_all(summed, "dec", split_axis=0, concat_axis=0, tiled=True)


def body_general(
    queries,
    new_kv,
    kv_pool,
    block_table,
    lengths,
    new_group,
    hidden_rows,
    norm_gain,
    routes,
    route_logits,
    w_gate,
    w_up,
    w_down,
):
    step_total = new_kv.shape[0]
    req_local = new_kv.shape[1]
    kv_width = new_kv.shape[3]
    block_local = kv_pool.shape[0]
    block_tokens = kv_pool.shape[1]
    blocks_per = block_table.shape[1]
    span_total = blocks_per * block_tokens
    kv_local = kv_width // HD
    request_ids = jnp.arange(req_local)
    flat_pool = kv_pool.reshape(block_local * block_tokens, 2, kv_width)
    for step_index in range(step_total):
        position = lengths + step_index
        target_rows = (
            block_table[request_ids, position // block_tokens] * block_tokens
            + position % block_tokens
        )
        flat_pool = flat_pool.at[target_rows].set(new_kv[step_index])
    pool_now = flat_pool.reshape(block_local, block_tokens, 2, kv_width)
    cached = pool_now[block_table].reshape(req_local, span_total, 2, kv_local, HD)
    keys_all = cached[:, :, 0]
    values_all = cached[:, :, 1]
    attn_out = jnp.stack(
        [
            attend_step(queries[step_index], keys_all, values_all, lengths, step_index)
            for step_index in range(step_total)
        ]
    )
    group_self = lax.axis_index("dec")
    group_count = lax.axis_size("dec")
    leaving = (new_group != group_self).astype(jnp.int32)
    depart_slot = jnp.argmax(leaving)
    destination = new_group[depart_slot]
    depart_blocks = block_table[depart_slot]
    outgoing = pool_now[depart_blocks].reshape(span_total, 2, kv_width)
    every_cache, every_dest = (
        lax.all_gather(outgoing[None], "dec", axis=0, tiled=True),
        lax.all_gather(destination.reshape(1), "dec", axis=0, tiled=True),
    )
    source = jnp.argmax((every_dest == group_self).astype(jnp.int32))
    incoming = lax.dynamic_index_in_dim(every_cache, source, 0, keepdims=False)
    pool_after = pool_now.at[depart_blocks].set(
        incoming.reshape(blocks_per, block_tokens, 2, kv_width)
    )
    top_count = routes.shape[2]
    capacity = min(req_local, 2 * ((req_local * top_count + group_count - 1) // group_count))
    owners = jnp.repeat(request_ids, top_count)
    moe_list = []
    for step_index in range(step_total):
        slot_index = slot_layout(routes[step_index], group_count, capacity)
        route_probs = jax.nn.softmax(route_logits[step_index], axis=-1)
        local_rows = hidden_rows[step_index]
        buffer = (
            jnp.zeros((group_count * capacity, local_rows.shape[1]), jnp.bfloat16)
            .at[slot_index]
            .set(local_rows[owners])
        )
        full_rows = lax.all_gather(
            lax.all_to_all(
                buffer.reshape(group_count, capacity, -1),
                "dec",
                split_axis=0,
                concat_axis=0,
                tiled=True,
            ),
            "tp",
            axis=2,
            tiled=True,
        )
        returned_rows = expert_apply(rms_scaled(full_rows, norm_gain), w_gate, w_up, w_down)
        picked = returned_rows.reshape(group_count * capacity, -1)[slot_index].astype(jnp.float32)
        weighted = picked * route_probs.reshape(-1, 1)
        moe_list.append(
            jnp.sum(weighted.reshape(req_local, top_count, -1), axis=1).astype(jnp.bfloat16)
        )
    moe_out = jnp.stack(moe_list)
    return (attn_out, moe_out, pool_after)


MESH = pl.DeviceIdType.MESH
F32 = jnp.float32
BF = jnp.bfloat16
SS, ZG, X1, Y1, X2, Y2, SIB, TP, RA, RB, RA2, RB2, RZ = range(13)
PIECE = 64
HEAD = 16


def exchange_kernel(
    hid, gain, routes, logits, out_cache, wg_hbm, wu_hbm, wd_hbm,
    moe_ref, inc_ref,
    wg, wu, wd, gath, ss_out, ss_in, act, acc, tp_out, tp_in,
    a_out, a_in, b_out, b_in, a2_out, a2_in, b2_out, b2_in, z_out, z_in,
    mig_in, mig_out, wsem, ssem, rsem, m_s1, m_r1, m_s2, m_r2, local_sem,
):
    me = lax.axis_index("dec")
    core = lax.axis_index("tp")
    x, y, z = me % 2, (me // 2) % 2, me // 4
    x_peer = me + 1 - 2 * x
    y_peer = me + 2 - 4 * y
    z_peers = [me, me + 4 - 8 * (z % 2), ((z + 2) % 4) * 4 + me % 4, (3 - z) * 4 + me % 4]
    half = hid.shape[2]
    quarter = half // 2
    count = 16

    barrier = pltpu.get_barrier_semaphore()
    for m in range(1, count):
        pl.semaphore_signal(barrier, inc=1, device_id={"dec": (me + m) % count}, device_id_type=MESH)
    pl.semaphore_signal(barrier, inc=1, device_id={"tp": 1 - core}, device_id_type=MESH)

    weights = [
        pltpu.make_async_copy(src.at[0], dst, wsem.at[i])
        for i, (src, dst) in enumerate(((wg_hbm, wg), (wu_hbm, wu), (wd_hbm, wd)))
    ]
    for copy in weights:
        copy.start()

    raw = jnp.concatenate([hid[t].astype(F32) for t in range(hid.shape[0])], axis=0)
    own_sum = jnp.sum(raw * raw, axis=-1, keepdims=True)
    ss_out[...] = jnp.broadcast_to(own_sum, ss_out.shape)
    pl.semaphore_wait(barrier, count)

    def remote(kind, q, src, dst, peer):
        return pltpu.make_async_remote_copy(
            src_ref=src, dst_ref=dst, send_sem=ssem.at[kind, q], recv_sem=rsem.at[kind, q],
            device_id=peer, device_id_type=MESH,
        )

    ss_copy = remote(SS, 0, ss_out, ss_in, {"tp": 1 - core})
    ss_copy.start()

    lane = lax.broadcasted_iota(jnp.int32, (raw.shape[0], 128), 1)
    logit = jnp.concatenate([logits[t] for t in range(hid.shape[0])], axis=0)
    route = jnp.concatenate([routes[t] for t in range(hid.shape[0])], axis=0)
    grown = jnp.exp(logit - jnp.max(logit, axis=-1, keepdims=True))
    prob = grown / jnp.sum(grown, axis=-1, keepdims=True)
    dense = jnp.zeros(lane.shape, F32)
    for k in range(route.shape[1]):
        hit = (lane % 16) == route[:, k : k + 1]
        dense = dense + jnp.where(hit, prob[:, k : k + 1], 0.0)
    high = dense.astype(BF)
    low = (dense - high.astype(F32)).astype(BF)
    packed = jnp.where(lane < 16, high.astype(F32), low.astype(F32)).astype(BF)

    ss_copy.wait()
    total = own_sum + ss_in[:, 0:1]
    factor = lax.rsqrt(total * (1.0 / (2 * half)) + eps_norm)
    own_gain = jnp.where(core == 0, gain[0:1], gain[1:2])
    rows = raw.shape[0]
    gath[core, 0, 0:rows, 0:half] = (raw * factor * own_gain).astype(BF)
    gath[core, 0, 0:rows, half:] = packed

    def slot(q, j, lo=0, hi=None):
        return gath.at[core, q, pl.ds(j * rows, rows), pl.ds(lo, (hi or gath.shape[3]) - lo)]

    sends = []

    def go(copy):
        copy.start()
        sends.append(copy)
        return copy

    x1, y1 = {}, {}

    def spread(q):
        x1[q] = go(remote(X1, q, slot(q, 0), slot(q, 1), {"dec": x_peer}))
        y1[q] = go(remote(Y1, q, slot(q, 0), slot(q, 2), {"dec": y_peer}))

    spread(0)
    zg = {q: go(remote(ZG, q, slot(0, 0), slot(q, 0), {"dec": z_peers[q]})) for q in (1, 2, 3)}

    first = []
    for m in range(1, count):
        peer = (me + m) % count
        copy = pltpu.make_async_remote_copy(
            src_ref=out_cache.at[peer], dst_ref=mig_in.at[m],
            send_sem=m_s1.at[m], recv_sem=m_r1.at[m], device_id={"dec": peer}, device_id_type=MESH,
        )
        copy.start()
        first.append(copy)
    mig_in[0] = out_cache[me]

    def gather(q):
        if q < 3:
            zg[q + 1].wait_recv()
            spread(q + 1)
        y1[q].wait_recv()
        x2 = go(remote(X2, q, slot(q, 2, 0, quarter), slot(q, 3, 0, quarter), {"dec": x_peer}))
        x1[q].wait_recv()
        y2 = go(remote(Y2, q, slot(q, 1, quarter), slot(q, 3, quarter), {"dec": y_peer}))
        x2.wait_recv()
        y2.wait_recv()
        return go(remote(SIB, q, gath.at[core, q], gath.at[core, q], {"tp": 1 - core}))

    def apply(q):
        if q == 0:
            weights[0].wait()
            weights[1].wait()

        @pl.loop(0, act.shape[1] // 256)
        def _(i):
            cols = pl.ds(pl.multiple_of(i * 256, 256), 256)

            def product(w):
                return jnp.dot(
                    gath[0, q, :, 0:half], w[0:half, cols], preferred_element_type=F32
                ) + jnp.dot(
                    gath[1, q, :, 0:half], w[half : 2 * half, cols], preferred_element_type=F32
                )

            g = product(wg)
            act[:, cols] = (g / (1.0 + jnp.exp(-g)) * product(wu)).astype(BF)

        if q == 0:
            weights[2].wait()
        probs = gath[0, q, :, half:].astype(F32)
        lanes = lax.broadcasted_iota(jnp.int32, probs.shape, 1)
        mine = (lanes == me) | (lanes == me + 16)
        weight = jnp.sum(jnp.where(mine, probs, 0.0), axis=-1, keepdims=True)
        step = 512

        @pl.loop(0, half // step)
        def _(i):
            to = pl.ds(pl.multiple_of(i * step, step), step)
            cols = pl.ds(pl.multiple_of((1 - core) * half + i * step, step), step)
            tp_out[q, :, to] = (
                jnp.dot(act[...], wd[:, cols], preferred_element_type=F32) * weight
            ).astype(BF)

        copy = go(remote(TP, q, tp_out.at[q], tp_in.at[q], {"tp": 1 - core}))

        @pl.loop(0, half // step)
        def _(i):
            to = pl.ds(pl.multiple_of(i * step, step), step)
            cols = pl.ds(pl.multiple_of(core * half + i * step, step), step)
            acc[q, :, to] = jnp.dot(act[...], wd[:, cols], preferred_element_type=F32) * weight

        return copy

    ra, rb, ra2, rb2, rz = {}, {}, {}, {}, {}
    r = rows

    def fold1(q, copy):
        copy.wait_recv()
        acc[q] = acc[q] + tp_in[q].astype(F32)
        a_out[q, 0:r] = acc[q, r : 2 * r, 0:quarter].astype(BF)
        a_out[q, r : 2 * r] = acc[q, 3 * r : 4 * r, 0:quarter].astype(BF)
        ra[q] = go(remote(RA, q, a_out.at[q], a_in.at[q], {"dec": x_peer}))
        b_out[q] = acc[q, 2 * r : 4 * r, quarter:].astype(BF)
        rb[q] = go(remote(RB, q, b_out.at[q], b_in.at[q], {"dec": y_peer}))

    def fold2(q):
        ra[q].wait_recv()
        a2_out[q] = (acc[q, 2 * r : 3 * r, 0:quarter] + a_in[q, r : 2 * r].astype(F32)).astype(BF)
        ra2[q] = go(remote(RA2, q, a2_out.at[q], a2_in.at[q], {"dec": y_peer}))
        rb[q].wait_recv()
        b2_out[q] = (acc[q, r : 2 * r, quarter:] + b_in[q, r : 2 * r].astype(F32)).astype(BF)
        rb2[q] = go(remote(RB2, q, b2_out.at[q], b2_in.at[q], {"dec": x_peer}))
        acc[q, 0:r, 0:quarter] = acc[q, 0:r, 0:quarter] + a_in[q, 0:r].astype(F32)
        acc[q, 0:r, quarter:] = acc[q, 0:r, quarter:] + b_in[q, 0:r].astype(F32)

    def fold3(q):
        ra2[q].wait_recv()
        rb2[q].wait_recv()
        acc[q, 0:r, 0:quarter] = acc[q, 0:r, 0:quarter] + a2_in[q].astype(F32)
        acc[q, 0:r, quarter:] = acc[q, 0:r, quarter:] + b2_in[q].astype(F32)
        if q:
            z_out[q] = acc[q, 0:r].astype(BF)
            rz[q] = go(remote(RZ, q, z_out.at[q], z_in.at[q], {"dec": z_peers[q]}))

    sib = gather(0)
    for copy in first:
        copy.wait()
    width = mig_out.shape[2]
    second = []
    for m in range(count):
        peer = (me + m) % count
        wanted = peer.astype(F32)
        chosen = jnp.zeros((PIECE, width), F32)
        for n in range(count):
            head = mig_in[n, PIECE:, :].astype(F32)[0:1]
            chosen = jnp.where(head == wanted, mig_in[n, 0:PIECE].astype(F32), chosen)
        mig_out[m] = chosen.astype(BF)
        where = inc_ref.at[pl.ds(me * PIECE, PIECE)]
        if m:
            copy = pltpu.make_async_remote_copy(
                src_ref=mig_out.at[m], dst_ref=where, send_sem=m_s2.at[m], recv_sem=m_r2.at[m],
                device_id={"dec": peer}, device_id_type=MESH,
            )
        else:
            copy = pltpu.make_async_copy(mig_out.at[m], where, local_sem)
        copy.start()
        second.append(copy)

    sib.wait_recv()
    tp0 = apply(0)
    sib = gather(1)
    fold1(0, tp0)
    sib.wait_recv()
    tp1 = apply(1)
    fold2(0)
    sib = gather(2)
    fold1(1, tp1)
    fold3(0)
    sib.wait_recv()
    tp2 = apply(2)
    fold2(1)
    sib = gather(3)
    fold1(2, tp2)
    fold3(1)
    sib.wait_recv()
    tp3 = apply(3)
    fold2(2)
    fold1(3, tp3)
    fold3(2)
    fold2(3)
    for copy in second:
        copy.wait()
    fold3(3)
    result = acc[0, 0:r]
    for q in (1, 2, 3):
        rz[q].wait_recv()
        result = result + z_in[q].astype(F32)
    for t in range(moe_ref.shape[0]):
        moe_ref[t] = result[t * 8 : t * 8 + 8].astype(BF)
    for copy in sends:
        copy.wait_send()


def exchange(hidden, gain, routes, logits, out_cache, w_gate, w_up, w_down):
    steps, req, half = hidden.shape
    rows = steps * req
    quarter = half // 2
    wide = w_gate.shape[2]
    vm = pltpu.VMEM
    scratch = [
        vm(w_gate.shape[1:], BF), vm(w_up.shape[1:], BF), vm(w_down.shape[1:], BF),
        vm((2, 4, 4 * rows, half + 128), BF),
        vm((rows, 128), F32), vm((rows, 128), F32),
        vm((4 * rows, wide), BF),
        vm((4, 4 * rows, half), F32),
        vm((4, 4 * rows, half), BF), vm((4, 4 * rows, half), BF),
        vm((4, 2 * rows, quarter), BF), vm((4, 2 * rows, quarter), BF),
        vm((4, 2 * rows, quarter), BF), vm((4, 2 * rows, quarter), BF),
        vm((4, rows, quarter), BF), vm((4, rows, quarter), BF),
        vm((4, rows, quarter), BF), vm((4, rows, quarter), BF),
        vm((4, rows, half), BF), vm((4, rows, half), BF),
        vm(out_cache.shape, BF), vm((16, PIECE, 128), BF),
        pltpu.SemaphoreType.DMA((3,)),
        pltpu.SemaphoreType.DMA((13, 4)), pltpu.SemaphoreType.DMA((13, 4)),
        pltpu.SemaphoreType.DMA((16,)), pltpu.SemaphoreType.DMA((16,)),
        pltpu.SemaphoreType.DMA((16,)), pltpu.SemaphoreType.DMA((16,)),
        pltpu.SemaphoreType.DMA,
    ]
    inside = pl.BlockSpec(memory_space=pltpu.VMEM)
    outside = pl.BlockSpec(memory_space=pl.ANY)
    return pl.pallas_call(
        exchange_kernel,
        out_shape=(
            jax.ShapeDtypeStruct((steps, req, half), BF),
            jax.ShapeDtypeStruct((16 * PIECE, 128), BF),
        ),
        in_specs=[inside] * 5 + [outside] * 3,
        out_specs=(inside, inside),
        scratch_shapes=scratch,
        compiler_params=pltpu.CompilerParams(
            collective_id=0, has_side_effects=True, vmem_limit_bytes=56 * 1024 * 1024
        ),
    )(hidden, gain, routes, logits, out_cache, w_gate, w_up, w_down)


def leaving_slot(moves):
    me = lax.axis_index("dec")
    slot = jnp.int32(0)
    for r in range(1, moves.shape[0]):
        slot = jnp.where(moves[r] != me, r, slot)
    return slot


def cache_kernel(
    table, lengths, moves, q_ref, new_ref, pool, attn_ref, pool_out, outgoing,
    cache, q_wide, o_wide, read_sem, write_sem,
):
    req, blocks = table.shape
    rows = cache.shape[1] // blocks
    reads = [[None] * blocks for _ in range(req)]
    for r in range(req):
        for j in range(blocks):
            at = pl.ds(pl.multiple_of(table[r, j] * rows, rows), rows)
            reads[r][j] = pltpu.make_async_copy(
                pool.at[at], cache.at[r, pl.ds(j * rows, rows)], read_sem.at[r, j]
            )
            reads[r][j].start()
    q_wide[...] = q_ref[...].reshape(q_wide.shape).astype(F32)
    heads = q_ref.shape[1]
    steps = q_ref.shape[0]
    kv_local = 2
    shape = (steps * heads, cache.shape[1])
    row = lax.broadcasted_iota(jnp.int32, shape, 0)
    col = lax.broadcasted_iota(jnp.int32, shape, 1)
    matching = (col % 4) == 2 * ((row % heads) // (heads // kv_local))
    offset = jnp.where(matching, col // 4 - row // heads, 1 << 20)
    part = lax.broadcasted_iota(jnp.int32, (16, 128), 0) // 4
    writes = []
    for r in range(req):
        for j in range(blocks):
            reads[r][j].wait()
        for t in range(steps):
            place = lengths[r] + t
            window = pl.ds(pl.multiple_of((place // 4) * 16, 16), 16)
            old = cache[r, window].astype(F32)
            cache[r, window] = jnp.where(part == place % 4, new_ref[t, r], old).astype(BF)
        for j in range(blocks):
            at = pl.ds(pl.multiple_of(table[r, j] * rows, rows), rows)
            copy = pltpu.make_async_copy(
                cache.at[r, pl.ds(j * rows, rows)], pool_out.at[at], write_sem.at[r, j]
            )
            copy.start()
            writes.append(copy)
    slot = leaving_slot(moves)
    target = moves[slot].astype(F32)
    for n in range(outgoing.shape[0]):
        outgoing[n, 0:PIECE] = cache[slot, pl.ds(n * PIECE, PIECE)]
        outgoing[n, PIECE:] = jnp.full((HEAD, 128), target, F32).astype(BF)
    for r in range(req):
        kv = cache[r]
        query = q_wide[pl.ds(r, steps * heads, stride=req), :].astype(BF)
        scores = lax.dot_general(
            query, kv, (((1,), (1,)), ((), ())), preferred_element_type=F32
        ) * (1.0 / math.sqrt(HD))
        visible = offset < lengths[r] + 1
        masked = jnp.where(visible, scores, -1e30)
        grown = jnp.where(visible, jnp.exp(masked - jnp.max(masked, axis=-1, keepdims=True)), 0.0)
        shares = grown / jnp.sum(grown, axis=-1, keepdims=True)
        shares = pltpu.roll(shares, 1, 1).astype(BF)
        o_wide[pl.ds(r, steps * heads, stride=req), :] = jnp.dot(
            shares, kv, preferred_element_type=F32
        )
    attn_ref[...] = o_wide[...].astype(BF).reshape(attn_ref.shape)
    for copy in writes:
        copy.wait()


def place_kernel(table, moves, incoming, pool, pool_out, sem):
    del pool
    slot = leaving_slot(moves)
    blocks = table.shape[1]
    rows = incoming.shape[0] // blocks
    copies = []
    for j in range(blocks):
        at = pl.ds(pl.multiple_of(table[slot, j] * rows, rows), rows)
        copy = pltpu.make_async_copy(incoming.at[pl.ds(j * rows, rows)], pool_out.at[at], sem.at[j])
        copy.start()
        copies.append(copy)
    for copy in copies:
        copy.wait()


def dense_rows(values):
    lead = values.shape[:-2]
    n = len(lead)
    split = values.reshape(*lead, 2, values.shape[-1] // HD, HD)
    return split.transpose(*range(n), n + 1, n, n + 2)


def body_slots(
    queries, new_kv, kv_pool, block_table, lengths, new_group, hidden_rows, norm_gain,
    routes, route_logits, w_gate, w_up, w_down,
):
    steps, req, _, kv_width = new_kv.shape
    blocks, block_tokens = kv_pool.shape[:2]
    span_rows = block_table.shape[1] * block_tokens * 4
    heads = queries.shape[2] // HD
    pool = dense_rows(kv_pool).reshape(-1, HD)
    new = jnp.tile(dense_rows(new_kv).reshape(steps, req, 4, HD), (1, 1, 4, 1)).astype(F32)
    q = queries.reshape(steps, req, heads, HD).transpose(0, 2, 1, 3)
    scalar = pl.BlockSpec(memory_space=pltpu.SMEM)
    inside = pl.BlockSpec(memory_space=pltpu.VMEM)
    outside = pl.BlockSpec(memory_space=pl.ANY)
    attn, pool_now, outgoing = pl.pallas_call(
        cache_kernel,
        out_shape=(
            jax.ShapeDtypeStruct(q.shape, BF),
            jax.ShapeDtypeStruct(pool.shape, BF),
            jax.ShapeDtypeStruct((16, PIECE + HEAD, HD), BF),
        ),
        in_specs=[scalar] * 3 + [inside] * 2 + [outside],
        out_specs=(inside, outside, inside),
        scratch_shapes=[
            pltpu.VMEM((req, span_rows, HD), BF),
            pltpu.VMEM((steps * heads * req, HD), F32),
            pltpu.VMEM((steps * heads * req, HD), F32),
            pltpu.SemaphoreType.DMA(block_table.shape),
            pltpu.SemaphoreType.DMA(block_table.shape),
        ],
        compiler_params=pltpu.CompilerParams(vmem_limit_bytes=32 * 1024 * 1024),
    )(block_table, lengths, new_group, q, new, pool)
    moe_out, incoming = exchange(
        hidden_rows, norm_gain.astype(F32).reshape(2, -1), routes, route_logits,
        outgoing, w_gate, w_up, w_down,
    )
    pool_after = pl.pallas_call(
        place_kernel,
        out_shape=jax.ShapeDtypeStruct(pool.shape, BF),
        in_specs=[scalar] * 2 + [outside] * 2,
        out_specs=outside,
        scratch_shapes=[pltpu.SemaphoreType.DMA((block_table.shape[1],))],
        input_output_aliases={3: 0},
    )(block_table, new_group, incoming, pool_now)
    back = pool_after.reshape(blocks, block_tokens, kv_width // HD, 2, HD)
    pool_after = back.transpose(0, 1, 3, 2, 4).reshape(kv_pool.shape)
    attn_out = attn.transpose(0, 2, 1, 3).reshape(queries.shape)
    return attn_out, moe_out, pool_after


def solution(mesh):
    sized = mesh.shape["dec"] == 16 and mesh.shape["tp"] == 2
    body = body_slots if sized else body_general
    return jax.shard_map(
        body,
        mesh=mesh,
        in_specs=(
            P(None, "dec", "tp"),
            P(None, "dec", None, "tp"),
            P("dec", None, None, "tp"),
            P("dec", None),
            P("dec"),
            P("dec"),
            P(None, "dec", "tp"),
            P(),
            P(None, "dec", None),
            P(None, "dec", None),
            P("dec", None, "tp"),
            P("dec", None, "tp"),
            P("dec", "tp", None),
        ),
        out_specs=(P(None, "dec", "tp"), P(None, "dec", "tp"), P("dec", None, None, "tp")),
        check_vma=False,
    )
```

```python
import math

import jax
import jax.numpy as jnp
from jax import lax
from jax.experimental import pallas as pl
from jax.experimental.pallas import tpu as pltpu
from jax.sharding import PartitionSpec as P

HD = 128


eps_norm = 1e-06


def rms_scaled(values, gain_vec):
    widened = values.astype(jnp.float32)
    factor = lax.rsqrt(jnp.mean(widened * widened, axis=-1, keepdims=True) + eps_norm)
    return (widened * factor * gain_vec.astype(jnp.float32)).astype(jnp.bfloat16)


def attend_step(query_rows, keys_all, values_all, lengths, step_index):
    row_count, cache_span, kv_local, head_dim = keys_all.shape
    group_ratio = query_rows.shape[1] // (kv_local * head_dim)
    grouped = query_rows.reshape(row_count, kv_local, group_ratio, head_dim)
    scores = jnp.einsum("rkgd,rlkd->rkgl", grouped, keys_all, preferred_element_type=jnp.float32)
    scores = scores * (1.0 / math.sqrt(head_dim))
    visible = jnp.arange(cache_span)[None, :] < (lengths + step_index + 1)[:, None]
    visible = visible[:, None, None, :]
    masked = jnp.where(visible, scores, -1e30)
    highest = jnp.max(masked, axis=-1, keepdims=True)
    weights = jnp.where(visible, jnp.exp(masked - highest), 0.0)
    weight_sum = jnp.sum(weights, axis=-1, keepdims=True)
    shares = (weights / weight_sum).astype(jnp.bfloat16)
    mixed_out = jnp.einsum(
        "rkgl,rlkd->rkgd", shares, values_all, preferred_element_type=jnp.float32
    )
    return mixed_out.astype(jnp.bfloat16).reshape(row_count, -1)


def slot_layout(route_ids, experts_all, capacity):
    flat_ids = route_ids.reshape(-1)
    hits_table = (flat_ids[:, None] == jnp.arange(experts_all)[None, :]).astype(jnp.int32)
    earlier = jnp.cumsum(hits_table, axis=0) - hits_table
    placing = jnp.sum(earlier * hits_table, axis=1)
    return flat_ids * capacity + placing


def expert_apply(normed, w_gate, w_up, w_down):
    flat_rows = normed.reshape(-1, normed.shape[-1])
    gate_out = jnp.dot(flat_rows, w_gate[0], preferred_element_type=jnp.float32)
    up_out = jnp.dot(flat_rows, w_up[0], preferred_element_type=jnp.float32)
    inner_act = (jax.nn.silu(gate_out) * up_out).astype(jnp.bfloat16)
    partial_value = jnp.dot(inner_act, w_down[0], preferred_element_type=jnp.float32)
    partial_value = partial_value.reshape(normed.shape[0], normed.shape[1], -1)
    summed = lax.psum_scatter(partial_value, "tp", scatter_dimension=2, tiled=True).astype(
        jnp.bfloat16
    )
    return lax.all_to_all(summed, "dec", split_axis=0, concat_axis=0, tiled=True)


def body_general(
    queries,
    new_kv,
    kv_pool,
    block_table,
    lengths,
    new_group,
    hidden_rows,
    norm_gain,
    routes,
    route_logits,
    w_gate,
    w_up,
    w_down,
):
    step_total = new_kv.shape[0]
    req_local = new_kv.shape[1]
    kv_width = new_kv.shape[3]
    block_local = kv_pool.shape[0]
    block_tokens = kv_pool.shape[1]
    blocks_per = block_table.shape[1]
    span_total = blocks_per * block_tokens
    kv_local = kv_width // HD
    request_ids = jnp.arange(req_local)
    flat_pool = kv_pool.reshape(block_local * block_tokens, 2, kv_width)
    for step_index in range(step_total):
        position = lengths + step_index
        target_rows = (
            block_table[request_ids, position // block_tokens] * block_tokens
            + position % block_tokens
        )
        flat_pool = flat_pool.at[target_rows].set(new_kv[step_index])
    pool_now = flat_pool.reshape(block_local, block_tokens, 2, kv_width)
    cached = pool_now[block_table].reshape(req_local, span_total, 2, kv_local, HD)
    keys_all = cached[:, :, 0]
    values_all = cached[:, :, 1]
    attn_out = jnp.stack(
        [
            attend_step(queries[step_index], keys_all, values_all, lengths, step_index)
            for step_index in range(step_total)
        ]
    )
    group_self = lax.axis_index("dec")
    group_count = lax.axis_size("dec")
    leaving = (new_group != group_self).astype(jnp.int32)
    depart_slot = jnp.argmax(leaving)
    destination = new_group[depart_slot]
    depart_blocks = block_table[depart_slot]
    outgoing = pool_now[depart_blocks].reshape(span_total, 2, kv_width)
    every_cache, every_dest = (
        lax.all_gather(outgoing[None], "dec", axis=0, tiled=True),
        lax.all_gather(destination.reshape(1), "dec", axis=0, tiled=True),
    )
    source = jnp.argmax((every_dest == group_self).astype(jnp.int32))
    incoming = lax.dynamic_index_in_dim(every_cache, source, 0, keepdims=False)
    pool_after = pool_now.at[depart_blocks].set(
        incoming.reshape(blocks_per, block_tokens, 2, kv_width)
    )
    top_count = routes.shape[2]
    capacity = min(req_local, 2 * ((req_local * top_count + group_count - 1) // group_count))
    owners = jnp.repeat(request_ids, top_count)
    moe_list = []
    for step_index in range(step_total):
        slot_index = slot_layout(routes[step_index], group_count, capacity)
        route_probs = jax.nn.softmax(route_logits[step_index], axis=-1)
        local_rows = hidden_rows[step_index]
        buffer = (
            jnp.zeros((group_count * capacity, local_rows.shape[1]), jnp.bfloat16)
            .at[slot_index]
            .set(local_rows[owners])
        )
        full_rows = lax.all_gather(
            lax.all_to_all(
                buffer.reshape(group_count, capacity, -1),
                "dec",
                split_axis=0,
                concat_axis=0,
                tiled=True,
            ),
            "tp",
            axis=2,
            tiled=True,
        )
        returned_rows = expert_apply(rms_scaled(full_rows, norm_gain), w_gate, w_up, w_down)
        picked = returned_rows.reshape(group_count * capacity, -1)[slot_index].astype(jnp.float32)
        weighted = picked * route_probs.reshape(-1, 1)
        moe_list.append(
            jnp.sum(weighted.reshape(req_local, top_count, -1), axis=1).astype(jnp.bfloat16)
        )
    moe_out = jnp.stack(moe_list)
    return (attn_out, moe_out, pool_after)


MESH = pl.DeviceIdType.MESH
F32 = jnp.float32
BF = jnp.bfloat16
SS, ZG, X1, Y1, X2, Y2, SIB, TP, RA, RB, RA2, RB2, RZ = range(13)
SIBS = (SIB, 13, 14, 15)
PIECE = 64
HEAD = 16


def exchange_kernel(
    hid, gain, routes, logits, out_cache, wg_hbm, wu_hbm, wd_hbm,
    moe_ref, inc_ref,
    wg, wu, wd, gath, ss_out, ss_in, act, acc, tp_out, tp_in,
    a_out, a_in, b_out, b_in, a2_out, a2_in, b2_out, b2_in, z_out, z_in,
    mig_in, mig_out, wsem, ssem, rsem, m_s1, m_r1, m_s2, m_r2, local_sem,
):
    me = lax.axis_index("dec")
    core = lax.axis_index("tp")
    x, y, z = me % 2, (me // 2) % 2, me // 4
    x_peer = me + 1 - 2 * x
    y_peer = me + 2 - 4 * y
    z_peers = [me, me + 4 - 8 * (z % 2), ((z + 2) % 4) * 4 + me % 4, (3 - z) * 4 + me % 4]
    half = hid.shape[2]
    quarter = half // 2
    count = 16

    barrier = pltpu.get_barrier_semaphore()
    for m in range(1, count):
        pl.semaphore_signal(barrier, inc=1, device_id={"dec": (me + m) % count}, device_id_type=MESH)
    pl.semaphore_signal(barrier, inc=1, device_id={"tp": 1 - core}, device_id_type=MESH)

    weights = [
        pltpu.make_async_copy(src.at[0], dst, wsem.at[i])
        for i, (src, dst) in enumerate(((wg_hbm, wg), (wu_hbm, wu), (wd_hbm, wd)))
    ]
    for copy in weights:
        copy.start()

    raw = jnp.concatenate([hid[t].astype(F32) for t in range(hid.shape[0])], axis=0)
    own_sum = jnp.sum(raw * raw, axis=-1, keepdims=True)
    ss_out[...] = jnp.broadcast_to(own_sum, ss_out.shape)
    pl.semaphore_wait(barrier, count)

    def remote(kind, q, src, dst, peer):
        return pltpu.make_async_remote_copy(
            src_ref=src, dst_ref=dst, send_sem=ssem.at[kind, q], recv_sem=rsem.at[kind, q],
            device_id=peer, device_id_type=MESH,
        )

    ss_copy = remote(SS, 0, ss_out, ss_in, {"tp": 1 - core})
    ss_copy.start()

    lane = lax.broadcasted_iota(jnp.int32, (raw.shape[0], 128), 1)
    logit = jnp.concatenate([logits[t] for t in range(hid.shape[0])], axis=0)
    route = jnp.concatenate([routes[t] for t in range(hid.shape[0])], axis=0)
    grown = jnp.exp(logit - jnp.max(logit, axis=-1, keepdims=True))
    prob = grown / jnp.sum(grown, axis=-1, keepdims=True)
    dense = jnp.zeros(lane.shape, F32)
    for k in range(route.shape[1]):
        hit = (lane % 16) == route[:, k : k + 1]
        dense = dense + jnp.where(hit, prob[:, k : k + 1], 0.0)
    high = dense.astype(BF)
    low = (dense - high.astype(F32)).astype(BF)
    packed = jnp.where(lane < 16, high.astype(F32), low.astype(F32)).astype(BF)

    ss_copy.wait()
    total = own_sum + ss_in[:, 0:1]
    factor = lax.rsqrt(total * (1.0 / (2 * half)) + eps_norm)
    own_gain = jnp.where(core == 0, gain[0:1], gain[1:2])
    rows = raw.shape[0]
    gath[core, 0, 0:rows, 0:half] = (raw * factor * own_gain).astype(BF)
    gath[core, 0, 0:rows, half:] = packed

    def slot(q, j, lo=0, hi=None):
        return gath.at[core, q, pl.ds(j * rows, rows), pl.ds(lo, (hi or gath.shape[3]) - lo)]

    sends = []

    def go(copy):
        copy.start()
        sends.append(copy)
        return copy

    x1, y1 = {}, {}

    def spread(q):
        x1[q] = go(remote(X1, q, slot(q, 0), slot(q, 1), {"dec": x_peer}))
        y1[q] = go(remote(Y1, q, slot(q, 0), slot(q, 2), {"dec": y_peer}))

    spread(0)
    zg = {q: go(remote(ZG, q, slot(0, 0), slot(q, 0), {"dec": z_peers[q]})) for q in (1, 2, 3)}

    def relay(q, n):
        part = slot(q, n)
        return go(remote(SIBS[n], q, part, part, {"tp": 1 - core}))

    relays, crossed = {}, {}

    def gather_a(q):
        relays[q] = [relay(q, 0)]
        y1[q].wait_recv()
        x2 = go(remote(X2, q, slot(q, 2, 0, quarter), slot(q, 3, 0, quarter), {"dec": x_peer}))
        x1[q].wait_recv()
        y2 = go(remote(Y2, q, slot(q, 1, quarter), slot(q, 3, quarter), {"dec": y_peer}))
        crossed[q] = (x2, y2)
        relays[q] += [relay(q, 1), relay(q, 2)]
        if q < 3:
            zg[q + 1].wait_recv()
            spread(q + 1)

    def gather_b(q):
        for copy in crossed[q]:
            copy.wait_recv()
        relays[q].append(relay(q, 3))
        for copy in relays[q]:
            copy.wait_recv()

    def apply(q):
        if q == 0:
            weights[0].wait()
            weights[1].wait()

        @pl.loop(0, act.shape[1] // 256)
        def _(i):
            cols = pl.ds(pl.multiple_of(i * 256, 256), 256)

            def product(w):
                return jnp.dot(
                    gath[0, q, :, 0:half], w[0:half, cols], preferred_element_type=F32
                ) + jnp.dot(
                    gath[1, q, :, 0:half], w[half : 2 * half, cols], preferred_element_type=F32
                )

            g = product(wg)
            act[:, cols] = (g / (1.0 + jnp.exp(-g)) * product(wu)).astype(BF)

        if q == 0:
            weights[2].wait()
        probs = gath[0, q, :, half:].astype(F32)
        lanes = lax.broadcasted_iota(jnp.int32, probs.shape, 1)
        mine = (lanes == me) | (lanes == me + 16)
        weight = jnp.sum(jnp.where(mine, probs, 0.0), axis=-1, keepdims=True)
        step = 512

        @pl.loop(0, half // step)
        def _(i):
            to = pl.ds(pl.multiple_of(i * step, step), step)
            cols = pl.ds(pl.multiple_of((1 - core) * half + i * step, step), step)
            tp_out[q, :, to] = (
                jnp.dot(act[...], wd[:, cols], preferred_element_type=F32) * weight
            ).astype(BF)

        copy = go(remote(TP, q, tp_out.at[q], tp_in.at[q], {"tp": 1 - core}))

        @pl.loop(0, half // step)
        def _(i):
            to = pl.ds(pl.multiple_of(i * step, step), step)
            cols = pl.ds(pl.multiple_of(core * half + i * step, step), step)
            acc[q, :, to] = jnp.dot(act[...], wd[:, cols], preferred_element_type=F32) * weight

        return copy

    ra, rb, ra2, rb2, rz = {}, {}, {}, {}, {}
    r = rows

    def fold1(q, copy):
        copy.wait_recv()
        acc[q] = acc[q] + tp_in[q].astype(F32)
        a_out[q, 0:r] = acc[q, r : 2 * r, 0:quarter].astype(BF)
        a_out[q, r : 2 * r] = acc[q, 3 * r : 4 * r, 0:quarter].astype(BF)
        ra[q] = go(remote(RA, q, a_out.at[q], a_in.at[q], {"dec": x_peer}))
        b_out[q] = acc[q, 2 * r : 4 * r, quarter:].astype(BF)
        rb[q] = go(remote(RB, q, b_out.at[q], b_in.at[q], {"dec": y_peer}))

    def fold2(q):
        ra[q].wait_recv()
        a2_out[q] = (acc[q, 2 * r : 3 * r, 0:quarter] + a_in[q, r : 2 * r].astype(F32)).astype(BF)
        ra2[q] = go(remote(RA2, q, a2_out.at[q], a2_in.at[q], {"dec": y_peer}))
        rb[q].wait_recv()
        b2_out[q] = (acc[q, r : 2 * r, quarter:] + b_in[q, r : 2 * r].astype(F32)).astype(BF)
        rb2[q] = go(remote(RB2, q, b2_out.at[q], b2_in.at[q], {"dec": x_peer}))
        acc[q, 0:r, 0:quarter] = acc[q, 0:r, 0:quarter] + a_in[q, 0:r].astype(F32)
        acc[q, 0:r, quarter:] = acc[q, 0:r, quarter:] + b_in[q, 0:r].astype(F32)

    def fold3(q):
        ra2[q].wait_recv()
        rb2[q].wait_recv()
        acc[q, 0:r, 0:quarter] = acc[q, 0:r, 0:quarter] + a2_in[q].astype(F32)
        acc[q, 0:r, quarter:] = acc[q, 0:r, quarter:] + b2_in[q].astype(F32)
        if q:
            z_out[q] = acc[q, 0:r].astype(BF)
            rz[q] = go(remote(RZ, q, z_out.at[q], z_in.at[q], {"dec": z_peers[q]}))

    gather_a(0)
    first = []
    for m in range(1, count):
        peer = (me + m) % count
        copy = pltpu.make_async_remote_copy(
            src_ref=out_cache.at[peer], dst_ref=mig_in.at[m],
            send_sem=m_s1.at[m], recv_sem=m_r1.at[m], device_id={"dec": peer}, device_id_type=MESH,
        )
        copy.start()
        first.append(copy)
    mig_in[0] = out_cache[me]

    gather_b(0)
    tp0 = apply(0)
    gather_a(1)
    fold1(0, tp0)
    gather_b(1)
    tp1 = apply(1)
    gather_a(2)
    fold1(1, tp1)
    fold2(0)
    for copy in first:
        copy.wait()
    width = mig_out.shape[2]
    second = []
    for m in range(count):
        peer = (me + m) % count
        wanted = peer.astype(F32)
        chosen = jnp.zeros((PIECE, width), F32)
        for n in range(count):
            head = mig_in[n, PIECE:, :].astype(F32)[0:1]
            chosen = jnp.where(head == wanted, mig_in[n, 0:PIECE].astype(F32), chosen)
        mig_out[m] = chosen.astype(BF)
        where = inc_ref.at[pl.ds(me * PIECE, PIECE)]
        if m:
            copy = pltpu.make_async_remote_copy(
                src_ref=mig_out.at[m], dst_ref=where, send_sem=m_s2.at[m], recv_sem=m_r2.at[m],
                device_id={"dec": peer}, device_id_type=MESH,
            )
        else:
            copy = pltpu.make_async_copy(mig_out.at[m], where, local_sem)
        copy.start()
        second.append(copy)


    gather_b(2)
    tp2 = apply(2)
    gather_a(3)
    fold1(2, tp2)
    fold2(1)
    fold3(0)
    gather_b(3)
    tp3 = apply(3)
    fold2(2)
    fold1(3, tp3)
    fold3(1)
    fold3(2)
    fold2(3)
    for copy in second:
        copy.wait()
    fold3(3)
    result = acc[0, 0:r]
    for q in (1, 2, 3):
        rz[q].wait_recv()
        result = result + z_in[q].astype(F32)
    for t in range(moe_ref.shape[0]):
        moe_ref[t] = result[t * 8 : t * 8 + 8].astype(BF)
    for copy in sends:
        copy.wait_send()


def exchange(hidden, gain, routes, logits, out_cache, w_gate, w_up, w_down):
    steps, req, half = hidden.shape
    rows = steps * req
    quarter = half // 2
    wide = w_gate.shape[2]
    vm = pltpu.VMEM
    scratch = [
        vm(w_gate.shape[1:], BF), vm(w_up.shape[1:], BF), vm(w_down.shape[1:], BF),
        vm((2, 4, 4 * rows, half + 128), BF),
        vm((rows, 128), F32), vm((rows, 128), F32),
        vm((4 * rows, wide), BF),
        vm((4, 4 * rows, half), F32),
        vm((4, 4 * rows, half), BF), vm((4, 4 * rows, half), BF),
        vm((4, 2 * rows, quarter), BF), vm((4, 2 * rows, quarter), BF),
        vm((4, 2 * rows, quarter), BF), vm((4, 2 * rows, quarter), BF),
        vm((4, rows, quarter), BF), vm((4, rows, quarter), BF),
        vm((4, rows, quarter), BF), vm((4, rows, quarter), BF),
        vm((4, rows, half), BF), vm((4, rows, half), BF),
        vm(out_cache.shape, BF), vm((16, PIECE, 128), BF),
        pltpu.SemaphoreType.DMA((3,)),
        pltpu.SemaphoreType.DMA((16, 4)), pltpu.SemaphoreType.DMA((16, 4)),
        pltpu.SemaphoreType.DMA((16,)), pltpu.SemaphoreType.DMA((16,)),
        pltpu.SemaphoreType.DMA((16,)), pltpu.SemaphoreType.DMA((16,)),
        pltpu.SemaphoreType.DMA,
    ]
    inside = pl.BlockSpec(memory_space=pltpu.VMEM)
    outside = pl.BlockSpec(memory_space=pl.ANY)
    return pl.pallas_call(
        exchange_kernel,
        out_shape=(
            jax.ShapeDtypeStruct((steps, req, half), BF),
            jax.ShapeDtypeStruct((16 * PIECE, 128), BF),
        ),
        in_specs=[inside] * 5 + [outside] * 3,
        out_specs=(inside, inside),
        scratch_shapes=scratch,
        compiler_params=pltpu.CompilerParams(
            collective_id=0, has_side_effects=True, vmem_limit_bytes=56 * 1024 * 1024
        ),
    )(hidden, gain, routes, logits, out_cache, w_gate, w_up, w_down)


def leaving_slot(moves):
    me = lax.axis_index("dec")
    slot = jnp.int32(0)
    for r in range(1, moves.shape[0]):
        slot = jnp.where(moves[r] != me, r, slot)
    return slot


def cache_kernel(
    table, lengths, moves, q_ref, new_ref, pool, attn_ref, pool_out, outgoing,
    cache, q_wide, o_wide, read_sem, write_sem,
):
    req, blocks = table.shape
    rows = cache.shape[1] // blocks
    reads = [[None] * blocks for _ in range(req)]
    for r in range(req):
        for j in range(blocks):
            at = pl.ds(pl.multiple_of(table[r, j] * rows, rows), rows)
            reads[r][j] = pltpu.make_async_copy(
                pool.at[at], cache.at[r, pl.ds(j * rows, rows)], read_sem.at[r, j]
            )
            reads[r][j].start()
    q_wide[...] = q_ref[...].reshape(q_wide.shape).astype(F32)
    heads = q_ref.shape[1]
    steps = q_ref.shape[0]
    kv_local = 2
    shape = (steps * heads, cache.shape[1])
    row = lax.broadcasted_iota(jnp.int32, shape, 0)
    col = lax.broadcasted_iota(jnp.int32, shape, 1)
    matching = (col % 4) == 2 * ((row % heads) // (heads // kv_local))
    offset = jnp.where(matching, col // 4 - row // heads, 1 << 20)
    part = lax.broadcasted_iota(jnp.int32, (16, 128), 0) // 4
    writes = []
    for r in range(req):
        for j in range(blocks):
            reads[r][j].wait()
        for t in range(steps):
            place = lengths[r] + t
            window = pl.ds(pl.multiple_of((place // 4) * 16, 16), 16)
            old = cache[r, window].astype(F32)
            cache[r, window] = jnp.where(part == place % 4, new_ref[t, r], old).astype(BF)
        for j in range(blocks):
            at = pl.ds(pl.multiple_of(table[r, j] * rows, rows), rows)
            copy = pltpu.make_async_copy(
                cache.at[r, pl.ds(j * rows, rows)], pool_out.at[at], write_sem.at[r, j]
            )
            copy.start()
            writes.append(copy)
    slot = leaving_slot(moves)
    target = moves[slot].astype(F32)
    for n in range(outgoing.shape[0]):
        outgoing[n, 0:PIECE] = cache[slot, pl.ds(n * PIECE, PIECE)]
        outgoing[n, PIECE:] = jnp.full((HEAD, 128), target, F32).astype(BF)
    for r in range(req):
        kv = cache[r]
        query = q_wide[pl.ds(r, steps * heads, stride=req), :].astype(BF)
        scores = lax.dot_general(
            query, kv, (((1,), (1,)), ((), ())), preferred_element_type=F32
        ) * (1.0 / math.sqrt(HD))
        visible = offset < lengths[r] + 1
        masked = jnp.where(visible, scores, -1e30)
        grown = jnp.where(visible, jnp.exp(masked - jnp.max(masked, axis=-1, keepdims=True)), 0.0)
        shares = grown / jnp.sum(grown, axis=-1, keepdims=True)
        shares = pltpu.roll(shares, 1, 1).astype(BF)
        o_wide[pl.ds(r, steps * heads, stride=req), :] = jnp.dot(
            shares, kv, preferred_element_type=F32
        )
    attn_ref[...] = o_wide[...].astype(BF).reshape(attn_ref.shape)
    for copy in writes:
        copy.wait()


def place_kernel(table, moves, incoming, pool, pool_out, sem):
    del pool
    slot = leaving_slot(moves)
    blocks = table.shape[1]
    rows = incoming.shape[0] // blocks
    copies = []
    for j in range(blocks):
        at = pl.ds(pl.multiple_of(table[slot, j] * rows, rows), rows)
        copy = pltpu.make_async_copy(incoming.at[pl.ds(j * rows, rows)], pool_out.at[at], sem.at[j])
        copy.start()
        copies.append(copy)
    for copy in copies:
        copy.wait()


def dense_rows(values):
    lead = values.shape[:-2]
    n = len(lead)
    split = values.reshape(*lead, 2, values.shape[-1] // HD, HD)
    return split.transpose(*range(n), n + 1, n, n + 2)


def body_slots(
    queries, new_kv, kv_pool, block_table, lengths, new_group, hidden_rows, norm_gain,
    routes, route_logits, w_gate, w_up, w_down,
):
    steps, req, _, kv_width = new_kv.shape
    blocks, block_tokens = kv_pool.shape[:2]
    span_rows = block_table.shape[1] * block_tokens * 4
    heads = queries.shape[2] // HD
    pool = dense_rows(kv_pool).reshape(-1, HD)
    new = jnp.tile(dense_rows(new_kv).reshape(steps, req, 4, HD), (1, 1, 4, 1)).astype(F32)
    q = queries.reshape(steps, req, heads, HD).transpose(0, 2, 1, 3)
    scalar = pl.BlockSpec(memory_space=pltpu.SMEM)
    inside = pl.BlockSpec(memory_space=pltpu.VMEM)
    outside = pl.BlockSpec(memory_space=pl.ANY)
    attn, pool_now, outgoing = pl.pallas_call(
        cache_kernel,
        out_shape=(
            jax.ShapeDtypeStruct(q.shape, BF),
            jax.ShapeDtypeStruct(pool.shape, BF),
            jax.ShapeDtypeStruct((16, PIECE + HEAD, HD), BF),
        ),
        in_specs=[scalar] * 3 + [inside] * 2 + [outside],
        out_specs=(inside, outside, inside),
        scratch_shapes=[
            pltpu.VMEM((req, span_rows, HD), BF),
            pltpu.VMEM((steps * heads * req, HD), F32),
            pltpu.VMEM((steps * heads * req, HD), F32),
            pltpu.SemaphoreType.DMA(block_table.shape),
            pltpu.SemaphoreType.DMA(block_table.shape),
        ],
        compiler_params=pltpu.CompilerParams(vmem_limit_bytes=56 * 1024 * 1024),
    )(block_table, lengths, new_group, q, new, pool)
    moe_out, incoming = exchange(
        hidden_rows, norm_gain.astype(F32).reshape(2, -1), routes, route_logits,
        outgoing, w_gate, w_up, w_down,
    )
    pool_after = pl.pallas_call(
        place_kernel,
        out_shape=jax.ShapeDtypeStruct(pool.shape, BF),
        in_specs=[scalar] * 2 + [inside, outside],
        out_specs=outside,
        scratch_shapes=[pltpu.SemaphoreType.DMA((block_table.shape[1],))],
        input_output_aliases={3: 0},
        compiler_params=pltpu.CompilerParams(vmem_limit_bytes=56 * 1024 * 1024),
    )(block_table, new_group, incoming, pool_now)
    back = pool_after.reshape(blocks, block_tokens, kv_width // HD, 2, HD)
    pool_after = back.transpose(0, 1, 3, 2, 4).reshape(kv_pool.shape)
    attn_out = attn.transpose(0, 2, 1, 3).reshape(queries.shape)
    return attn_out, moe_out, pool_after


def solution(mesh):
    sized = mesh.shape["dec"] == 16 and mesh.shape["tp"] == 2
    body = body_slots if sized else body_general
    return jax.shard_map(
        body,
        mesh=mesh,
        in_specs=(
            P(None, "dec", "tp"),
            P(None, "dec", None, "tp"),
            P("dec", None, None, "tp"),
            P("dec", None),
            P("dec"),
            P("dec"),
            P(None, "dec", "tp"),
            P(),
            P(None, "dec", None),
            P(None, "dec", None),
            P("dec", None, "tp"),
            P("dec", None, "tp"),
            P("dec", "tp", None),
        ),
        out_specs=(P(None, "dec", "tp"), P(None, "dec", "tp"), P("dec", None, None, "tp")),
        check_vma=False,
    )
```
